128 devices in a mesh: dp: 4 (over y), seq: 32 (over x, z, core).
Axes of the slice: x: 4, y: 4, z: 4, core: 2. Of those that a mesh axis runs over, the one named last changes fastest.
Arguments:
- queries: bfloat16 [16384, 4096], P(('dp', 'seq')), parts along dimension 0, may hold values from -6 to 6
- key_codes: bfloat16 [16384, 1024], P(('dp', 'seq')), parts along dimension 0, may hold values from -6 to 6
- key_block_scale: bfloat16 [128, 8], P(('dp', 'seq')), parts along dimension 0, may hold values from 0.5 to 2
- value_code_matrix: bfloat16 [16384, 1024], P(('dp', 'seq')), parts along dimension 0, may hold values from -6 to 6
- value_block_scale: bfloat16 [128, 8], P(('dp', 'seq')), parts along dimension 0, may hold values from 0.5 to 2
- attn_out: bfloat16 [16384, 4096], P(('dp', 'seq')), parts along dimension 0, may hold values from -4 to 4
- out_grad: bfloat16 [16384, 4096], P(('dp', 'seq')), parts along dimension 0, may hold values from -6 to 6
Outputs:
- query_grad: bfloat16 [16384, 4096], P(('dp', 'seq')), parts along dimension 0
- dequant_key_gradient: bfloat16 [16384, 1024], P(('dp', 'seq')), parts along dimension 0
- dequant_value_gradient: bfloat16 [16384, 1024], P(('dp', 'seq')), parts along dimension 0
The draws below stay inside these ranges and needn't reach their ends.
There are 4 independent parts, one for each index of `dp`. The reference program is written for one: setup_inputs(seed, part) draws one part's arguments, and reference() takes and returns one part's arrays. A program takes and returns all parts, laid end to end along the dimension named above; each array names one. Nothing has to cross between parts.
All inputs are finite; a program needn't handle non-finite values.
Results may differ from the reference program's by a relative error of at most 0.0014.
The reference program's roundings to bfloat16 on the way count: a program that leaves them out, or rounds other values in their place, can miss the bound.
Values may be sent and summed in bfloat16 or wider, within the bound.
A program may use at most 128 MiB of HBM per device.

```python
import math
import jax
import jax.numpy as jnp
from jax import lax

QUERY_HEADS = 32
KEY_VALUE_HEADS = 8
HEAD_WIDTH = 128
SCALE_BLOCK_SPAN = 128
SEQUENCE_LENGTH = 4096


def draw_queries(key, part):
    key = jax.random.fold_in(key, 11)
    dimension_list = (SEQUENCE_LENGTH, QUERY_HEADS, HEAD_WIDTH)
    random_sample = jnp.clip(jax.random.normal(key, dimension_list, jnp.float32), -6.0, 6.0)
    return random_sample.reshape(SEQUENCE_LENGTH, QUERY_HEADS * HEAD_WIDTH).astype(jnp.bfloat16)


def draw_key_codes(key, part):
    key = jax.random.fold_in(key, 12)
    dimension_list = (SEQUENCE_LENGTH, KEY_VALUE_HEADS, HEAD_WIDTH)
    random_sample = jnp.clip(jax.random.normal(key, dimension_list, jnp.float32), -6.0, 6.0)
    return random_sample.reshape(SEQUENCE_LENGTH, KEY_VALUE_HEADS * HEAD_WIDTH).astype(jnp.bfloat16)


def block_scale(rng, dims, pieces, least, largest):
    level, own = 1.0, jax.random.fold_in(rng, 6)
    for position, parts in pieces:
        heights = jnp.exp(jax.random.uniform(jax.random.fold_in(own, position), (parts,), jnp.float32, least / len(pieces), largest / len(pieces)))
        level = level * jnp.repeat(heights, dims[position] // parts).reshape([-1 if axis == position else 1 for axis in range(len(dims))])
    return level


def noise(stream_key, extent, width, most, pieces=(), kind=jnp.bfloat16):
    level = block_scale(stream_key, extent, pieces, -0.22, 0.18) if pieces else 1.0
    array = jax.random.normal(stream_key, extent, jnp.float32) * width * level
    return jnp.minimum(jnp.maximum(array, -most), most).astype(kind)


def setup_inputs(seed: int = 0, part: int = 0) -> dict:
    streams_of = jax.random.split(jax.random.key(seed), 8)
    part_splits = jax.random.split(jax.random.fold_in(streams_of[7], part), 8)
    return {
        "queries": draw_queries(jax.random.fold_in(jax.random.fold_in(streams_of[7], part), 71), part),
        "key_codes": draw_key_codes(jax.random.fold_in(jax.random.fold_in(streams_of[7], part), 71), part),
        "key_block_scale": jnp.clip(jnp.exp(math.log(2.0) - 1.3862944 * jax.random.uniform(part_splits[2], (SEQUENCE_LENGTH // SCALE_BLOCK_SPAN, KEY_VALUE_HEADS), jnp.float32) ** block_scale(part_splits[2], (SEQUENCE_LENGTH // SCALE_BLOCK_SPAN, KEY_VALUE_HEADS), ((0, 32),), -0.2, 0.2)), 0.5, 2.0).astype(jnp.bfloat16),
        "value_code_matrix": noise(part_splits[3], (SEQUENCE_LENGTH, KEY_VALUE_HEADS * HEAD_WIDTH), 1.0, 6.0, ((0, 32),)),
        "value_block_scale": jnp.clip(jnp.exp(math.log(2.0) - 1.3862944 * jax.random.uniform(part_splits[4], (SEQUENCE_LENGTH // SCALE_BLOCK_SPAN, KEY_VALUE_HEADS), jnp.float32) ** block_scale(part_splits[4], (SEQUENCE_LENGTH // SCALE_BLOCK_SPAN, KEY_VALUE_HEADS), ((0, 32),), -0.2, 0.2)), 0.5, 2.0).astype(jnp.bfloat16),
        "attn_out": noise(part_splits[5], (SEQUENCE_LENGTH, QUERY_HEADS * HEAD_WIDTH), 0.3, 4.0, ((0, 32),)),
        "out_grad": noise(part_splits[6], (SEQUENCE_LENGTH, QUERY_HEADS * HEAD_WIDTH), 1.0, 6.0, ((0, 32),)),
    }


def dequantize(code_entries, scales):
    block_groups = code_entries.astype(jnp.float32).reshape(SEQUENCE_LENGTH // SCALE_BLOCK_SPAN, SCALE_BLOCK_SPAN, KEY_VALUE_HEADS, HEAD_WIDTH)
    block_groups = block_groups * scales.astype(jnp.float32)[:, None, :, None]
    return block_groups.reshape(SEQUENCE_LENGTH, KEY_VALUE_HEADS, HEAD_WIDTH).astype(jnp.bfloat16)


def reference(queries, key_codes, key_block_scale, value_code_matrix, value_block_scale, attn_out, out_grad):
    key_full = dequantize(key_codes, key_block_scale)
    value_full = dequantize(value_code_matrix, value_block_scale)
    query_heads = queries.reshape(SEQUENCE_LENGTH, QUERY_HEADS, HEAD_WIDTH)
    grad_heads = out_grad.reshape(SEQUENCE_LENGTH, QUERY_HEADS, HEAD_WIDTH)
    out_heads = attn_out.reshape(SEQUENCE_LENGTH, QUERY_HEADS, HEAD_WIDTH)
    row_delta = jnp.sum(grad_heads.astype(jnp.float32) * out_heads.astype(jnp.float32), axis=2)
    softmax_scale = HEAD_WIDTH ** -0.5
    positions = jnp.arange(SEQUENCE_LENGTH, dtype=jnp.int32)
    causal = positions[:, None] >= positions[None, :]
    query_group_count = QUERY_HEADS // KEY_VALUE_HEADS

    def one_head(head_num):
        kv_group = head_num // query_group_count
        query_one = lax.dynamic_index_in_dim(query_heads, head_num, 1, keepdims=False)
        grad_one = lax.dynamic_index_in_dim(grad_heads, head_num, 1, keepdims=False)
        key_one = lax.dynamic_index_in_dim(key_full, kv_group, 1, keepdims=False)
        value_one = lax.dynamic_index_in_dim(value_full, kv_group, 1, keepdims=False)
        delta_one = lax.dynamic_index_in_dim(row_delta, head_num, 1, keepdims=False)
        scores = jnp.dot(query_one, key_one.T, preferred_element_type=jnp.float32) * softmax_scale
        scores = jnp.where(causal, scores, -jnp.inf)
        row_max = jnp.max(scores, axis=1, keepdims=True)
        expo = jnp.exp(scores - row_max)
        row_total = jnp.sum(expo, axis=1, keepdims=True)
        attn_prob = expo / row_total
        prob_bf = attn_prob.astype(jnp.bfloat16)
        value_part = jnp.dot(prob_bf.T, grad_one, preferred_element_type=jnp.float32)
        prob_grad = jnp.dot(grad_one, value_one.T, preferred_element_type=jnp.float32)
        score_grad = (attn_prob * (prob_grad - delta_one[:, None]) * softmax_scale).astype(jnp.bfloat16)
        query_part = jnp.dot(score_grad, key_one, preferred_element_type=jnp.float32).astype(jnp.bfloat16)
        key_part = jnp.dot(score_grad.T, query_one, preferred_element_type=jnp.float32)
        return query_part, key_part, value_part

    query_all, gathered_keys, gathered_values = lax.map(one_head, jnp.arange(QUERY_HEADS, dtype=jnp.int32))
    query_grad = jnp.transpose(query_all, (1, 0, 2)).reshape(SEQUENCE_LENGTH, QUERY_HEADS * HEAD_WIDTH)
    key_gradient_total = jnp.sum(gathered_keys.reshape(KEY_VALUE_HEADS, query_group_count, SEQUENCE_LENGTH, HEAD_WIDTH), axis=1)
    value_gradient_total = jnp.sum(gathered_values.reshape(KEY_VALUE_HEADS, query_group_count, SEQUENCE_LENGTH, HEAD_WIDTH), axis=1)
    dequant_key_gradient = jnp.transpose(key_gradient_total, (1, 0, 2)).reshape(SEQUENCE_LENGTH, KEY_VALUE_HEADS * HEAD_WIDTH).astype(jnp.bfloat16)
    dequant_value_gradient = jnp.transpose(value_gradient_total, (1, 0, 2)).reshape(SEQUENCE_LENGTH, KEY_VALUE_HEADS * HEAD_WIDTH).astype(jnp.bfloat16)
    return (query_grad, dequant_key_gradient, dequant_value_gradient)
```

```python
import jax
import jax.numpy as jnp
from jax import lax
from jax.experimental import pallas as pl
from jax.experimental.pallas import tpu as pltpu
from jax.sharding import PartitionSpec as P

F32, BF = jnp.float32, jnp.bfloat16
W = 128
SC = W ** -0.5
C2 = SC * 1.4426950408889634
CH = 512
MESH = pl.DeviceIdType.MESH


def dot(a, b):
    return jnp.dot(a, b, preferred_element_type=F32)


def kernel(
    q_in, k_in, ks_in, v_in, vs_in, o_in, g_in,
    dq_out, dk_out, dv_out,
    gl, ol, kl, vl, ksl, vsl, dts, kvs,
    kv, kt, qbuf, gbuf, de,
    sbuf, qt, gt, qn, gn, dqt, ml,
    acc, dqs, rbuf1, fs, rbuf2, fb,
    lsem, s1s, kvr, f1s, f2s, f3s, qs, qr, gs, gr, des, der, dqss, dqr,
    r1s, r1r, r2s, r2r, dks, dvs, dkr, dvr,
):
    dp = lax.axis_index("dp")
    s = lax.axis_index("seq")
    x, z, core = s // 8, (s // 2) % 4, s % 2
    b = ((z + 1) // 2) % 2
    me = x * 4 + (z // 2) * 2 + core
    grp = me // 2
    other = s + 1 - 2 * core
    partner = x * 8 + (2 * (z // 2) + 1 - z % 2) * 2 + core

    def seq_in(n, bb):
        return (n // 4) * 8 + (bb + ((n // 2) % 2) * (3 - 2 * bb)) * 2 + n % 2

    def seq_of(n):
        return seq_in(n, b)

    def rcopy(src, dst, ssem, rsem, dev):
        return pltpu.make_async_remote_copy(
            src_ref=src, dst_ref=dst, send_sem=ssem, recv_sem=rsem,
            device_id=(dp, dev), device_id_type=MESH,
        )

    def arrived(dst, sem):
        pltpu.make_async_copy(dst, dst, sem).wait()

    def loop(n, f, start=0):
        def body(i, c):
            f(i)
            return c
        lax.fori_loop(start, n, body, 0)

    def cols(n, w):
        return pl.ds(pl.multiple_of(n * w, w), w)

    local = [
        pltpu.make_async_copy(a, c, lsem.at[i])
        for i, (a, c) in enumerate(
            ((k_in, kl), (ks_in, ksl), (v_in, vl), (vs_in, vsl), (g_in, gl), (o_in, ol))
        )
    ]
    for c in local:
        c.start()
    barrier = pltpu.get_barrier_semaphore()

    def greet(k):
        pl.semaphore_signal(
            barrier, inc=1, device_id=(dp, seq_of((me + k) % 16)), device_id_type=MESH
        )
    loop(16, greet, 1)
    pl.semaphore_signal(barrier, inc=1, device_id=(dp, partner), device_id_type=MESH)

    for c in local[:4]:
        c.wait()
    for i, (codes, scales) in enumerate(((kl, ksl), (vl, vsl))):
        sc = scales[...].astype(F32)
        for g in range(8):
            kvs[g, i] = (codes[:, W * g:W * g + W].astype(F32) * sc[0:1, g:g + 1]).astype(BF)
    for c in local[4:]:
        c.wait()
    lane = lax.broadcasted_iota(jnp.int32, (W, W), 1)
    dmat = jnp.zeros((W, W), F32)
    for h in range(32):
        hs = slice(W * h, W * h + W)
        prod = gl[:, hs].astype(F32) * ol[:, hs].astype(F32)
        dmat = jnp.where(lane == h, jnp.sum(prod, axis=1, keepdims=True), dmat)
    dts[...] = dmat.T

    pl.semaphore_wait(barrier, 16)

    def send_kv(k):
        g = (grp + k) % 8
        rcopy(kvs.at[g], kv.at[s], s1s.at[k], kvr.at[s], seq_of(g * 2 + core)).start()
    loop(8, send_kv, 1)
    pltpu.make_async_copy(kvs.at[grp], kv.at[s], kvr.at[s]).start()

    def send_rows(k):
        n = (me + k) % 16
        dev = seq_of(n)
        rcopy(q_in.at[:, cols(n, 256)], qbuf.at[me], qs.at[k], qr.at[me], dev).start()
        rcopy(g_in.at[:, cols(n, 256)], gbuf.at[me], gs.at[k], gr.at[me], dev).start()
        rcopy(dts.at[cols(n // 4, 8)], de.at[me], des.at[k], der.at[me], dev).start()
    loop(16, send_rows, 1)
    pltpu.make_async_copy(q_in.at[:, cols(me, 256)], qbuf.at[me], qr.at[me]).start()
    pltpu.make_async_copy(g_in.at[:, cols(me, 256)], gbuf.at[me], gr.at[me]).start()
    pltpu.make_async_copy(dts.at[cols(me // 4, 8)], de.at[me], der.at[me]).start()

    def forward(k):
        j = seq_of(((grp + k) % 8) * 2 + core)
        arrived(kv.at[j], kvr.at[j])
        rcopy(kv.at[j], kv.at[j], f1s.at[k], kvr.at[j], partner).start()
        rcopy(kv.at[j], kv.at[j], f2s.at[k], kvr.at[j], other).start()
    loop(8, forward)

    def row(t):
        return seq_of(15 - t)

    def prep(u):
        w = u % 2
        for p in range(2):
            n = 15 - 2 * u - p
            arrived(qbuf.at[n], qr.at[n])
            arrived(gbuf.at[n], gr.at[n])
            arrived(de.at[n], der.at[n])
            for h in range(2):
                i = 2 * p + h
                q = qbuf[n, :, W * h:W * h + W]
                g = gbuf[n, :, W * h:W * h + W]
                qn[w, W * i:W * i + W, :] = q
                gn[w, W * i:W * i + W, :] = g
                qt[w, :, W * i:W * i + W] = q.T
                gt[w, :, W * i:W * i + W] = g.T
        ml[w, 0] = jnp.full((8, 512), -1e30, F32)
        ml[w, 1] = jnp.zeros((8, 512), F32)

    def chunk_of(i, c):
        return kv[pl.ds(4 * c, 4), i].reshape(CH, W)

    def stat(sv, w):
        m = ml[w, 0]
        s3 = sv.reshape(CH // 8, 8, 512)
        mn = jnp.maximum(m, jnp.max(s3, axis=0))
        ml[w, 1] = ml[w, 1] * jnp.exp2(m - mn) + jnp.sum(jnp.exp2(s3 - mn[None]), axis=0)
        ml[w, 0] = mn

    def part_a(c, u):
        w = u % 2
        sv = dot(chunk_of(0, c), qt[w]) * C2
        sbuf[w, cols(c, CH), :] = sv
        stat(sv, w)

    def last_a(u):
        w = u % 2
        c = 7 - u
        sv = dot(chunk_of(0, c), qt[w]) * C2
        kp = c * CH + lax.broadcasted_iota(jnp.int32, (CH, 512), 0)
        li = lax.broadcasted_iota(jnp.int32, (1, 512), 1)
        qp = jnp.where(li < 256, row(2 * u), row(2 * u + 1)) * W + (li & (W - 1))
        sv = jnp.where(kp <= qp, sv, -jnp.inf)
        sbuf[w, cols(c, CH), :] = sv
        stat(sv, w)

    def part_b(c, u, lse, delta):
        w = u % 2
        p = jnp.exp2(sbuf[w, cols(c, CH), :] - lse)
        dpr = dot(chunk_of(1, c), gt[w])
        ds = (p * (dpr - delta) * SC).astype(BF)
        pair = pl.ds(2 * c, 2)
        acc[1, pair] += dot(p.astype(BF), gn[w]).reshape(2, 2, W, W)
        acc[0, pair] += dot(ds, qn[w]).reshape(2, 2, W, W)
        dqt[...] += dot(kt[:, cols(c, CH)], ds)

    def begin(u):
        w = u % 2
        m, l = ml[w, 0], ml[w, 1]
        mm = jnp.max(m, axis=0, keepdims=True)
        lse = mm + jnp.log2(jnp.sum(l * jnp.exp2(m - mm), axis=0, keepdims=True))
        r0 = 2 * (me % 4)
        delta = jnp.concatenate(
            [de[15 - 2 * u - p, pl.ds(r0 + h, 1), :] for p in range(2) for h in range(2)], axis=1
        )
        dqt[...] = jnp.zeros((W, 512), F32)
        return lse, delta

    def stage1(c):
        rcopy(acc.at[:, pl.ds(2 * c, 2), 1 - core], rbuf1.at[c], r1s.at[c], r1r.at[c], other).start()

    def stage2(c):
        near = (c + b) % 2
        far = 1 - near
        arrived(rbuf1.at[c], r1r.at[c])
        for i in range(2):
            fs[c, i] = acc[i, 2 * c + far, core] + rbuf1[c, i, far]
        rcopy(fs.at[c], rbuf2.at[c], r2s.at[c], r2r.at[c], partner).start()
        for i in range(2):
            acc[i, 2 * c + near, core] += rbuf1[c, i, near]

    def stage3(c):
        near = (c + b) % 2
        own = c * 2 + core
        dev = seq_of(own)
        arrived(rbuf2.at[c], r2r.at[c])
        for i in range(2):
            fb[c, i] = (acc[i, 2 * c + near, core] + rbuf2[c, i]).astype(BF)
        for i, (out, ssem, rsem) in enumerate(((dk_out, dks, dkr), (dv_out, dvs, dvr))):
            dst = out.at[:, cols(grp, W)]

            @pl.when(own != me)
            def _():
                rcopy(fb.at[c, i], dst, ssem.at[c], rsem.at[grp], dev).start()

            @pl.when(own == me)
            def _():
                pltpu.make_async_copy(fb.at[c, i], dst, rsem.at[grp]).start()

    def end(u):
        for p in range(2):
            n = 15 - 2 * u - p
            for h in range(2):
                i = 2 * p + h
                dqs[n, :, W * h:W * h + W] = dqt[:, W * i:W * i + W].T.astype(BF)
            dst = dq_out.at[:, cols(me, 256)]

            @pl.when(n != me)
            def _():
                rcopy(dqs.at[n], dst, dqss.at[n], dqr.at[me], seq_of(n)).start()

            @pl.when(n == me)
            def _():
                pltpu.make_async_copy(dqs.at[n], dst, dqr.at[me]).start()
        stage1(7 - u)

        @pl.when(u >= 1)
        def _():
            stage2(8 - u)

        @pl.when(u >= 2)
        def _():
            stage3(9 - u)

    def clear(j):
        for i in range(2):
            acc[i, j] = jnp.zeros((2, W, W), F32)
    loop(16, clear)
    prep(0)

    def first(xx):
        for zz in range(2):
            j = seq_in(xx * 4 + zz * 2 + core, 1 - b)
            arrived(kv.at[j], kvr.at[j])
            rcopy(kv.at[j], kv.at[j], f3s.at[2 * xx + zz], kvr.at[j], other).start()
        for zz in range(4):
            j = xx * 8 + zz * 2 + 1 - core
            arrived(kv.at[j], kvr.at[j])
        for i in range(2):
            c = 2 * xx + i
            kt[:, cols(c, CH)] = chunk_of(0, c).T

        part_a(2 * xx, 0)

        @pl.when(xx < 3)
        def _():
            part_a(2 * xx + 1, 0)
    loop(4, first)
    last_a(0)

    def step(u):
        lse, delta = begin(u)
        prep(u + 1)

        def main(c):
            part_b(c, u, lse, delta)
            part_a(c, u + 1)
        loop(6 - u, main)
        part_b(6 - u, u, lse, delta)
        last_a(u + 1)
        part_b(7 - u, u, lse, delta)
        end(u)
    loop(7, step)
    lse, delta = begin(7)
    part_b(0, 7, lse, delta)
    end(7)
    stage2(0)
    stage3(1)
    stage3(0)

    def finish(n):
        arrived(dq_out.at[:, cols(n, 256)], dqr.at[n])

        @pl.when(n != me)
        def _():
            rcopy(dqs.at[n], dqs.at[n], dqss.at[n], dqr.at[n], other).wait_send()
    loop(16, finish)

    def finish8(c):
        arrived(dk_out.at[:, cols(c, W)], dkr.at[c])
        arrived(dv_out.at[:, cols(c, W)], dvr.at[c])
        rcopy(fs.at[c], fs.at[c], r2s.at[c], r2r.at[c], other).wait_send()
        rcopy(rbuf1.at[c], rbuf1.at[c], r1s.at[c], r1r.at[c], other).wait_send()
        rcopy(kv.at[0], kv.at[0], f1s.at[c], kvr.at[0], other).wait_send()
        rcopy(kv.at[0], kv.at[0], f2s.at[c], kvr.at[0], other).wait_send()
        rcopy(kv.at[0], kv.at[0], f3s.at[c], kvr.at[0], other).wait_send()

        @pl.when(c * 2 + core != me)
        def _():
            rcopy(fb.at[c, 0], fb.at[c, 0], dks.at[c], dkr.at[c], other).wait_send()
            rcopy(fb.at[c, 1], fb.at[c, 1], dvs.at[c], dvr.at[c], other).wait_send()

        @pl.when(c >= 1)
        def _():
            rcopy(kvs.at[0], kvs.at[0], s1s.at[c], kvr.at[0], other).wait_send()
    loop(8, finish8)

    def finish15(k):
        rcopy(qbuf.at[0], qbuf.at[0], qs.at[k], qr.at[0], other).wait_send()
        rcopy(gbuf.at[0], gbuf.at[0], gs.at[k], gr.at[0], other).wait_send()
        rcopy(de.at[0], de.at[0], des.at[k], der.at[0], other).wait_send()
    loop(16, finish15, 1)


def per_device(q, kc, ks, vc, vs, o, g):
    any_ = pl.BlockSpec(memory_space=pl.ANY)
    vm, dma = pltpu.VMEM, pltpu.SemaphoreType.DMA
    rows, qc = q.shape
    kc_cols = kc.shape[1]
    return pl.pallas_call(
        kernel,
        out_shape=[
            jax.ShapeDtypeStruct(q.shape, BF),
            jax.ShapeDtypeStruct(kc.shape, BF),
            jax.ShapeDtypeStruct(vc.shape, BF),
        ],
        in_specs=[any_] * 7,
        out_specs=[any_] * 3,
        scratch_shapes=[
            vm((rows, qc), BF), vm((rows, qc), BF), vm((rows, kc_cols), BF), vm((rows, kc_cols), BF),
            vm((1, 8), BF), vm((1, 8), BF), vm((W, W), F32), vm((8, 2, W, W), BF),
            vm((32, 2, W, W), BF), vm((W, 32 * W), BF),
            vm((16, W, 256), BF), vm((16, W, 256), BF), vm((16, 8, W), F32),
            vm((2, 32 * W, 512), F32),
            vm((2, W, 512), BF), vm((2, W, 512), BF), vm((2, 512, W), BF), vm((2, 512, W), BF),
            vm((W, 512), F32), vm((2, 2, 8, 512), F32),
            vm((2, 16, 2, W, W), F32), vm((16, W, 256), BF),
            vm((8, 2, 2, W, W), F32), vm((8, 2, W, W), F32), vm((8, 2, W, W), F32),
            vm((8, 2, W, W), BF),
            dma((6,)), dma((8,)), dma((32,)), dma((8,)), dma((8,)), dma((8,)),
            dma((16,)), dma((16,)), dma((16,)), dma((16,)), dma((16,)), dma((16,)),
            dma((16,)), dma((16,)),
            dma((8,)), dma((8,)), dma((8,)), dma((8,)), dma((8,)), dma((8,)), dma((8,)), dma((8,)),
        ],
        compiler_params=pltpu.CompilerParams(
            collective_id=0, has_side_effects=True, vmem_limit_bytes=56 * 2**20
        ),
        cost_estimate=pl.CostEstimate(
            flops=11_000_000_000, bytes_accessed=8_000_000, transcendentals=18_000_000
        ),
    )(q, kc, ks, vc, vs, o, g)


def solution(mesh):
    spec = P(("dp", "seq"), None)
    return jax.shard_map(
        per_device, mesh=mesh, in_specs=(spec,) * 7, out_specs=(spec,) * 3, check_vma=False
    )
```

```python
import jax
import jax.numpy as jnp
from jax import lax
from jax.experimental import pallas as pl
from jax.experimental.pallas import tpu as pltpu
from jax.sharding import PartitionSpec as P

F32, BF = jnp.float32, jnp.bfloat16
W = 128
SC = W ** -0.5
C2 = SC * 1.4426950408889634
CH = 512
MESH = pl.DeviceIdType.MESH
ROW_ORDER = (7, 0, 1, 2, 3, 4, 5, 6)
LAG2, LAG3 = 3, 14


def dot(a, b):
    return jnp.dot(a, b, preferred_element_type=F32)


def kernel(
    q_in, k_in, ks_in, v_in, vs_in, o_in, g_in,
    dq_out, dk_out, dv_out,
    gl, ol, kl, vl, ksl, vsl, dts, kvs,
    kv, kt, qbuf, gbuf, de,
    sbuf, qt, gt, qn, gn, dqt, ml, lse,
    acc, dqs, rbuf1, fs, rbuf2, fb,
    lsem, s1s, kvr, f1s, f2s, f3s, qs, qr, gs, gr, des, der, dqss, dqr,
    r1s, r1r, r2s, r2r, dks, dvs, dkr, dvr,
):
    dp = lax.axis_index("dp")
    s = lax.axis_index("seq")
    x, z, core = s // 8, (s // 2) % 4, s % 2
    b = ((z + 1) // 2) % 2
    me = x * 4 + (z // 2) * 2 + core
    grp = me // 2
    other = s + 1 - 2 * core
    partner = x * 8 + (2 * (z // 2) + 1 - z % 2) * 2 + core

    def seq_in(n, bb):
        return (n // 4) * 8 + (bb + ((n // 2) % 2) * (3 - 2 * bb)) * 2 + n % 2

    def seq_of(n):
        return seq_in(n, b)

    def rcopy(src, dst, ssem, rsem, dev):
        return pltpu.make_async_remote_copy(
            src_ref=src, dst_ref=dst, send_sem=ssem, recv_sem=rsem,
            device_id=(dp, dev), device_id_type=MESH,
        )

    def arrived(dst, sem):
        pltpu.make_async_copy(dst, dst, sem).wait()

    def loop(n, f, start=0):
        def body(i, c):
            f(i)
            return c
        lax.fori_loop(start, n, body, 0)

    def cols(n, w):
        return pl.ds(pl.multiple_of(n * w, w), w)

    local = [
        pltpu.make_async_copy(a, c, lsem.at[i])
        for i, (a, c) in enumerate(
            ((k_in, kl), (ks_in, ksl), (v_in, vl), (vs_in, vsl), (g_in, gl), (o_in, ol))
        )
    ]
    for c in local:
        c.start()
    barrier = pltpu.get_barrier_semaphore()

    def greet(k):
        pl.semaphore_signal(
            barrier, inc=1, device_id=(dp, seq_of((me + k) % 16)), device_id_type=MESH
        )
    loop(16, greet, 1)
    pl.semaphore_signal(barrier, inc=1, device_id=(dp, partner), device_id_type=MESH)

    for c in local[:4]:
        c.wait()
    for i, (codes, scales) in enumerate(((kl, ksl), (vl, vsl))):
        sc = scales[...].astype(F32)
        for g in range(8):
            kvs[g, i] = (codes[:, W * g:W * g + W].astype(F32) * sc[0:1, g:g + 1]).astype(BF)
    for c in local[4:]:
        c.wait()
    lane = lax.broadcasted_iota(jnp.int32, (W, W), 1)
    dmat = jnp.zeros((W, W), F32)
    for h in range(32):
        hs = slice(W * h, W * h + W)
        prod = gl[:, hs].astype(F32) * ol[:, hs].astype(F32)
        dmat = jnp.where(lane == h, jnp.sum(prod, axis=1, keepdims=True), dmat)
    dts[...] = dmat.T

    pl.semaphore_wait(barrier, 16)

    order = (1, 3, 2, 0)

    def group(xo, lo):
        return ((x + xo) % 4) * 2 + (grp + lo) % 2

    def send_kv(lo):
        for xo in order:
            g = group(xo, lo)

            def go():
                rcopy(kvs.at[g], kv.at[s], s1s.at[xo * 2 + lo], kvr.at[s], seq_of(g * 2 + core)).start()
            go() if xo else pl.when(lo > 0)(go)
    loop(2, send_kv)
    pltpu.make_async_copy(kvs.at[grp], kv.at[s], kvr.at[s]).start()

    def send_rows(src, dst, ssem, rsem):
        def send(lo):
            for xo in order:
                n = ((x + xo) % 4) * 4 + (me + lo) % 4

                def go():
                    rcopy(
                        src.at[:, cols(n, 256)], dst.at[me], ssem.at[xo * 4 + lo], rsem.at[me], seq_of(n)
                    ).start()
                go() if xo else pl.when(lo > 0)(go)
        loop(4, send)
        pltpu.make_async_copy(src.at[:, cols(me, 256)], dst.at[me], rsem.at[me]).start()

    def send_delta(k):
        n = (me + k) % 16
        rcopy(dts.at[cols(n // 4, 8)], de.at[me], des.at[k], der.at[me], seq_of(n)).start()
    def forward(lo):
        for xo in order:
            j = seq_of(group(4 - xo, lo) * 2 + core)
            k = xo * 2 + lo
            arrived(kv.at[j], kvr.at[j])
            rcopy(kv.at[j], kv.at[j], f1s.at[k], kvr.at[j], partner).start()
            rcopy(kv.at[j], kv.at[j], f2s.at[k], kvr.at[j], other).start()
    loop(2, forward)
    send_rows(q_in, qbuf, qs, qr)
    loop(16, send_delta, 1)
    pltpu.make_async_copy(dts.at[cols(me // 4, 8)], de.at[me], der.at[me]).start()

    def row(t):
        return seq_of(15 - t)

    def prep_a(u):
        for p in range(2):
            n = 15 - 2 * u - p
            arrived(qbuf.at[n], qr.at[n])
            for h in range(2):
                i = 2 * p + h
                qt[:, W * i:W * i + W] = qbuf[n, :, W * h:W * h + W].T
        ml[0] = jnp.full((8, 512), -1e30, F32)
        ml[1] = jnp.zeros((8, 512), F32)

    def prep_b(u):
        for p in range(2):
            n = 15 - 2 * u - p
            arrived(gbuf.at[n], gr.at[n])
            arrived(de.at[n], der.at[n])
            for h in range(2):
                i = 2 * p + h
                g = gbuf[n, :, W * h:W * h + W]
                qn[W * i:W * i + W, :] = qbuf[n, :, W * h:W * h + W]
                gn[W * i:W * i + W, :] = g
                gt[:, W * i:W * i + W] = g.T
        dqt[...] = jnp.zeros((W, 512), F32)

    def slot(u, c):
        return 8 * u - (u * (u - 1)) // 2 + c

    def chunk_of(i, c):
        return kv[pl.ds(4 * c, 4), i].reshape(CH, W)

    def stat(sv):
        m = ml[0]
        s3 = sv.reshape(CH // 8, 8, 512)
        mn = jnp.maximum(m, jnp.max(s3, axis=0))
        ml[1] = ml[1] * jnp.exp2(m - mn) + jnp.sum(jnp.exp2(s3 - mn[None]), axis=0)
        ml[0] = mn

    def part_a(c, u):
        sv = dot(chunk_of(0, c), qt[...]) * C2
        sbuf[slot(u, c)] = sv
        stat(sv)

    def last_a(u):
        c = 7 - u
        sv = dot(chunk_of(0, c), qt[...]) * C2
        kp = c * CH + lax.broadcasted_iota(jnp.int32, (CH, 512), 0)
        li = lax.broadcasted_iota(jnp.int32, (1, 512), 1)
        qp = jnp.where(li < 256, row(2 * u), row(2 * u + 1)) * W + (li & (W - 1))
        sv = jnp.where(kp <= qp, sv, -jnp.inf)
        sbuf[slot(u, c)] = sv
        stat(sv)
        m, l = ml[0], ml[1]
        mm = jnp.max(m, axis=0, keepdims=True)
        lse[u] = mm + jnp.log2(jnp.sum(l * jnp.exp2(m - mm), axis=0, keepdims=True))

    def part_b(c, u, delta):
        p = jnp.exp2(sbuf[slot(u, c)] - lse[u])
        dpr = dot(chunk_of(1, c), gt[...])
        ds = (p * (dpr - delta) * SC).astype(BF)
        pair = pl.ds(2 * c, 2)
        acc[1, pair] += dot(p.astype(BF), gn[...]).reshape(2, 2, W, W)
        acc[0, pair] += dot(ds, qn[...]).reshape(2, 2, W, W)
        dqt[...] += dot(kt[:, cols(c, CH)], ds)

    def delta_of(u):
        r0 = 2 * (me % 4)
        return jnp.concatenate(
            [de[15 - 2 * u - p, pl.ds(r0 + h, 1), :] for p in range(2) for h in range(2)], axis=1
        )

    def stage1(c):
        rcopy(acc.at[:, pl.ds(2 * c, 2), 1 - core], rbuf1.at[c], r1s.at[c], r1r.at[c], other).start()

    def stage2(c):
        near = (c + b) % 2
        far = 1 - near
        arrived(rbuf1.at[c], r1r.at[c])
        for i in range(2):
            fs[c, i] = acc[i, 2 * c + far, core] + rbuf1[c, i, far]
        rcopy(fs.at[c], rbuf2.at[c], r2s.at[c], r2r.at[c], partner).start()
        for i in range(2):
            acc[i, 2 * c + near, core] += rbuf1[c, i, near]

    def stage3(c):
        near = (c + b) % 2
        own = c * 2 + core
        dev = seq_of(own)
        arrived(rbuf2.at[c], r2r.at[c])
        for i in range(2):
            fb[c, i] = (acc[i, 2 * c + near, core] + rbuf2[c, i]).astype(BF)
        for i, (out, ssem, rsem) in enumerate(((dk_out, dks, dkr), (dv_out, dvs, dvr))):
            dst = out.at[:, cols(grp, W)]

            @pl.when(own != me)
            def _():
                rcopy(fb.at[c, i], dst, ssem.at[c], rsem.at[grp], dev).start()

            @pl.when(own == me)
            def _():
                pltpu.make_async_copy(fb.at[c, i], dst, rsem.at[grp]).start()

    def end(u):
        for p in range(2):
            n = 15 - 2 * u - p
            for h in range(2):
                i = 2 * p + h
                dqs[n, :, W * h:W * h + W] = dqt[:, W * i:W * i + W].T.astype(BF)
            dst = dq_out.at[:, cols(me, 256)]

            @pl.when(n != me)
            def _():
                rcopy(dqs.at[n], dst, dqss.at[n], dqr.at[me], seq_of(n)).start()

            @pl.when(n == me)
            def _():
                pltpu.make_async_copy(dqs.at[n], dst, dqr.at[me]).start()

    def clear(j):
        for i in range(2):
            acc[i, j] = jnp.zeros((2, W, W), F32)
    loop(16, clear)
    def first(xx):
        for zz in range(2):
            j = seq_in(xx * 4 + zz * 2 + core, 1 - b)
            arrived(kv.at[j], kvr.at[j])
            rcopy(kv.at[j], kv.at[j], f3s.at[2 * xx + zz], kvr.at[j], other).start()
        for zz in range(4):
            j = xx * 8 + zz * 2 + 1 - core
            arrived(kv.at[j], kvr.at[j])
        for i in range(2):
            c = 2 * xx + i
            kt[:, cols(c, CH)] = chunk_of(0, c).T
    loop(2, first)
    send_rows(g_in, gbuf, gs, gr)
    loop(4, first, 2)

    for u in range(7, -1, -1):
        prep_a(u)
        for c in range(7 - u):
            part_a(c, u)
        last_a(u)

    rows_done, due = set(), []
    cell = 0
    for u in ROW_ORDER:
        prep_b(u)
        delta = delta_of(u)
        rows_done.add(u)
        for c in range(7 - u, -1, -1):
            part_b(c, u, delta)
            cell += 1
            if all(r in rows_done for r in range(8 - c)):
                stage1(c)
                due.append((cell + LAG2, 2, c))
            for item in [d for d in due if d[0] <= cell]:
                due.remove(item)
                if item[1] == 2:
                    stage2(item[2])
                    due.append((cell + LAG3, 3, item[2]))
                else:
                    stage3(item[2])
        end(u)
    while due:
        due.sort()
        when, kind, c = due.pop(0)
        if kind == 2:
            stage2(c)
            due.append((when + LAG3, 3, c))
        else:
            stage3(c)

    def finish(n):
        arrived(dq_out.at[:, cols(n, 256)], dqr.at[n])

        @pl.when(n != me)
        def _():
            rcopy(dqs.at[n], dqs.at[n], dqss.at[n], dqr.at[n], other).wait_send()
    loop(16, finish)

    def finish8(c):
        arrived(dk_out.at[:, cols(c, W)], dkr.at[c])
        arrived(dv_out.at[:, cols(c, W)], dvr.at[c])
        rcopy(fs.at[c], fs.at[c], r2s.at[c], r2r.at[c], other).wait_send()
        rcopy(rbuf1.at[c], rbuf1.at[c], r1s.at[c], r1r.at[c], other).wait_send()
        rcopy(kv.at[0], kv.at[0], f1s.at[c], kvr.at[0], other).wait_send()
        rcopy(kv.at[0], kv.at[0], f2s.at[c], kvr.at[0], other).wait_send()
        rcopy(kv.at[0], kv.at[0], f3s.at[c], kvr.at[0], other).wait_send()

        @pl.when(c * 2 + core != me)
        def _():
            rcopy(fb.at[c, 0], fb.at[c, 0], dks.at[c], dkr.at[c], other).wait_send()
            rcopy(fb.at[c, 1], fb.at[c, 1], dvs.at[c], dvr.at[c], other).wait_send()

        @pl.when(c >= 1)
        def _():
            rcopy(kvs.at[0], kvs.at[0], s1s.at[c], kvr.at[0], other).wait_send()
    loop(8, finish8)

    def finish15(k):
        rcopy(qbuf.at[0], qbuf.at[0], qs.at[k], qr.at[0], other).wait_send()
        rcopy(gbuf.at[0], gbuf.at[0], gs.at[k], gr.at[0], other).wait_send()
        rcopy(de.at[0], de.at[0], des.at[k], der.at[0], other).wait_send()
    loop(16, finish15, 1)


def per_device(q, kc, ks, vc, vs, o, g):
    any_ = pl.BlockSpec(memory_space=pl.ANY)
    vm, dma = pltpu.VMEM, pltpu.SemaphoreType.DMA
    rows, qc = q.shape
    kc_cols = kc.shape[1]
    return pl.pallas_call(
        kernel,
        out_shape=[vm(q.shape, BF), vm(kc.shape, BF), vm(vc.shape, BF)],
        in_specs=[any_] * 7,
        out_specs=[pl.BlockSpec(memory_space=pltpu.VMEM)] * 3,
        scratch_shapes=[
            vm((rows, qc), BF), vm((rows, qc), BF), vm((rows, kc_cols), BF), vm((rows, kc_cols), BF),
            vm((1, 8), BF), vm((1, 8), BF), vm((W, W), F32), vm((8, 2, W, W), BF),
            vm((32, 2, W, W), BF), vm((W, 32 * W), BF),
            vm((16, W, 256), BF), vm((16, W, 256), BF), vm((16, 8, W), F32),
            vm((36, CH, 512), F32),
            vm((W, 512), BF), vm((W, 512), BF), vm((512, W), BF), vm((512, W), BF),
            vm((W, 512), F32), vm((2, 8, 512), F32), vm((8, 1, 512), F32),
            vm((2, 16, 2, W, W), F32), vm((16, W, 256), BF),
            vm((8, 2, 2, W, W), F32), vm((8, 2, W, W), F32), vm((8, 2, W, W), F32),
            vm((8, 2, W, W), BF),
            dma((6,)), dma((8,)), dma((32,)), dma((8,)), dma((8,)), dma((8,)),
            dma((16,)), dma((16,)), dma((16,)), dma((16,)), dma((16,)), dma((16,)),
            dma((16,)), dma((16,)),
            dma((8,)), dma((8,)), dma((8,)), dma((8,)), dma((8,)), dma((8,)), dma((8,)), dma((8,)),
        ],
        compiler_params=pltpu.CompilerParams(
            collective_id=0, has_side_effects=True, vmem_limit_bytes=62 * 2**20
        ),
        cost_estimate=pl.CostEstimate(
            flops=11_000_000_000, bytes_accessed=8_000_000, transcendentals=18_000_000
        ),
    )(q, kc, ks, vc, vs, o, g)


def solution(mesh):
    spec = P(("dp", "seq"), None)
    return jax.shard_map(
        per_device, mesh=mesh, in_specs=(spec,) * 7, out_specs=(spec,) * 3, check_vma=False
    )
```

```python
import jax
import jax.numpy as jnp
from jax import lax
from jax.experimental import pallas as pl
from jax.experimental.pallas import tpu as pltpu
from jax.sharding import PartitionSpec as P

F32, BF = jnp.float32, jnp.bfloat16
W = 128
SC = W ** -0.5
C2 = SC * 1.4426950408889634
CH = 512
MESH = pl.DeviceIdType.MESH


def dot(a, b):
    return jnp.dot(a, b, preferred_element_type=F32)


def kernel(
    q_in, k_in, ks_in, v_in, vs_in, o_in, g_in,
    dq_out, dk_out, dv_out,
    gl, ol, kl, vl, ksl, vsl, dts, kvs,
    kv, kt, qbuf, gbuf, de,
    sbuf, qt, gt, qn, gn, dqt, ml, lse,
    acc, dqs, rbuf1, fs, rbuf2, fb,
    lsem, s1s, kvr, f1s, f2s, f3s, qs, qr, gs, gr, des, der, dqss, dqr,
    r1s, r1r, r2s, r2r, dks, dvs, dkr, dvr,
):
    dp = lax.axis_index("dp")
    s = lax.axis_index("seq")
    x, z, core = s // 8, (s // 2) % 4, s % 2
    b = ((z + 1) // 2) % 2
    me = x * 4 + (z // 2) * 2 + core
    grp = me // 2
    other = s + 1 - 2 * core
    partner = x * 8 + (2 * (z // 2) + 1 - z % 2) * 2 + core

    def seq_in(n, bb):
        return (n // 4) * 8 + (bb + ((n // 2) % 2) * (3 - 2 * bb)) * 2 + n % 2

    def seq_of(n):
        return seq_in(n, b)

    def rcopy(src, dst, ssem, rsem, dev):
        return pltpu.make_async_remote_copy(
            src_ref=src, dst_ref=dst, send_sem=ssem, recv_sem=rsem,
            device_id=(dp, dev), device_id_type=MESH,
        )

    def arrived(dst, sem):
        pltpu.make_async_copy(dst, dst, sem).wait()

    def loop(n, f, start=0):
        def body(i, c):
            f(i)
            return c
        lax.fori_loop(start, n, body, 0)

    def cols(n, w):
        return pl.ds(pl.multiple_of(n * w, w), w)

    local = [
        pltpu.make_async_copy(a, c, lsem.at[i])
        for i, (a, c) in enumerate(
            ((k_in, kl), (ks_in, ksl), (v_in, vl), (vs_in, vsl), (g_in, gl), (o_in, ol))
        )
    ]
    for c in local:
        c.start()
    barrier = pltpu.get_barrier_semaphore()

    def greet(k):
        pl.semaphore_signal(
            barrier, inc=1, device_id=(dp, seq_of((me + k) % 16)), device_id_type=MESH
        )
    loop(16, greet, 1)
    pl.semaphore_signal(barrier, inc=1, device_id=(dp, partner), device_id_type=MESH)

    for c in local[:4]:
        c.wait()
    for i, (codes, scales) in enumerate(((kl, ksl), (vl, vsl))):
        sc = scales[...].astype(F32)
        for g in range(8):
            kvs[g, i] = (codes[:, W * g:W * g + W].astype(F32) * sc[0:1, g:g + 1]).astype(BF)
    for c in local[4:]:
        c.wait()
    lane = lax.broadcasted_iota(jnp.int32, (W, W), 1)
    dmat = jnp.zeros((W, W), F32)
    for h in range(32):
        hs = slice(W * h, W * h + W)
        prod = gl[:, hs].astype(F32) * ol[:, hs].astype(F32)
        dmat = jnp.where(lane == h, jnp.sum(prod, axis=1, keepdims=True), dmat)
    dts[...] = dmat.T

    pl.semaphore_wait(barrier, 16)

    order = (1, 3, 2, 0)

    def group(xo, lo):
        return ((x + xo) % 4) * 2 + (grp + lo) % 2

    def send_kv(lo):
        for xo in order:
            g = group(xo, lo)

            def go():
                rcopy(kvs.at[g], kv.at[s], s1s.at[xo * 2 + lo], kvr.at[s], seq_of(g * 2 + core)).start()
            go() if xo else pl.when(lo > 0)(go)
    loop(2, send_kv)
    pltpu.make_async_copy(kvs.at[grp], kv.at[s], kvr.at[s]).start()

    def send_rows(src, dst, ssem, rsem):
        def send(lo):
            for xo in order:
                n = ((x + xo) % 4) * 4 + (me + lo) % 4

                def go():
                    rcopy(
                        src.at[:, cols(n, 256)], dst.at[me], ssem.at[xo * 4 + lo], rsem.at[me], seq_of(n)
                    ).start()
                go() if xo else pl.when(lo > 0)(go)
        loop(4, send)
        pltpu.make_async_copy(src.at[:, cols(me, 256)], dst.at[me], rsem.at[me]).start()

    def send_delta(k):
        n = (me + k) % 16
        rcopy(dts.at[cols(n // 4, 8)], de.at[me], des.at[k], der.at[me], seq_of(n)).start()
    def forward(lo):
        for xo in order:
            j = seq_of(group(4 - xo, lo) * 2 + core)
            k = xo * 2 + lo
            arrived(kv.at[j], kvr.at[j])
            rcopy(kv.at[j], kv.at[j], f1s.at[k], kvr.at[j], partner).start()
            rcopy(kv.at[j], kv.at[j], f2s.at[k], kvr.at[j], other).start()
    loop(2, forward)
    send_rows(q_in, qbuf, qs, qr)
    loop(16, send_delta, 1)
    pltpu.make_async_copy(dts.at[cols(me // 4, 8)], de.at[me], der.at[me]).start()

    def row(t):
        return seq_of(15 - t)

    def prep_a(u):
        for p in range(2):
            n = 15 - 2 * u - p
            arrived(qbuf.at[n], qr.at[n])
            for h in range(2):
                i = 2 * p + h
                qt[:, W * i:W * i + W] = qbuf[n, :, W * h:W * h + W].T
        ml[0] = jnp.full((8, 512), -1e30, F32)
        ml[1] = jnp.zeros((8, 512), F32)

    def prep_b(u):
        for p in range(2):
            n = 15 - 2 * u - p
            arrived(gbuf.at[n], gr.at[n])
            arrived(de.at[n], der.at[n])
            for h in range(2):
                i = 2 * p + h
                g = gbuf[n, :, W * h:W * h + W]
                qn[W * i:W * i + W, :] = qbuf[n, :, W * h:W * h + W]
                gn[W * i:W * i + W, :] = g
                gt[:, W * i:W * i + W] = g.T
        dqt[...] = jnp.zeros((W, 512), F32)

    def slot(u, c):
        return 8 * u - (u * (u - 1)) // 2 + c

    def chunk_of(i, c, k=1):
        return kv[pl.ds(4 * c, 4 * k), i].reshape(k * CH, W)

    def stat(sv):
        m = ml[0]
        s3 = sv.reshape(CH // 8, 8, 512)
        mn = jnp.maximum(m, jnp.max(s3, axis=0))
        ml[1] = ml[1] * jnp.exp2(m - mn) + jnp.sum(jnp.exp2(s3 - mn[None]), axis=0)
        ml[0] = mn

    def part_a(c, u, k=1):
        for d in range(k):
            sv = dot(chunk_of(0, c + d), qt[...]) * C2
            sbuf[slot(u, c + d)] = sv
            stat(sv)

    def last_a(u):
        c = 7 - u
        sv = dot(chunk_of(0, c), qt[...]) * C2
        kp = c * CH + lax.broadcasted_iota(jnp.int32, (CH, 512), 0)
        li = lax.broadcasted_iota(jnp.int32, (1, 512), 1)
        qp = jnp.where(li < 256, row(2 * u), row(2 * u + 1)) * W + (li & (W - 1))
        sv = jnp.where(kp <= qp, sv, -jnp.inf)
        sbuf[slot(u, c)] = sv
        stat(sv)
        m, l = ml[0], ml[1]
        mm = jnp.max(m, axis=0, keepdims=True)
        lse[u] = mm + jnp.log2(jnp.sum(l * jnp.exp2(m - mm), axis=0, keepdims=True))

    def part_b(c, u, delta, k=1):
        p = jnp.exp2(sbuf[pl.ds(slot(u, c), k)].reshape(k * CH, 512) - lse[u])
        dpr = dot(chunk_of(1, c, k), gt[...])
        ds = (p * (dpr - delta) * SC).astype(BF)
        pair = pl.ds(2 * c, 2 * k)
        acc[1, pair] += dot(p.astype(BF), gn[...]).reshape(2 * k, 2, W, W)
        acc[0, pair] += dot(ds, qn[...]).reshape(2 * k, 2, W, W)
        dqt[...] += dot(kt[:, pl.ds(pl.multiple_of(c * CH, CH), k * CH)], ds)

    def delta_of(u):
        r0 = 2 * (me % 4)
        return jnp.concatenate(
            [de[15 - 2 * u - p, pl.ds(r0 + h, 1), :] for p in range(2) for h in range(2)], axis=1
        )

    def stage1(c):
        rcopy(acc.at[:, pl.ds(2 * c, 2), 1 - core], rbuf1.at[c], r1s.at[c], r1r.at[c], other).start()

    def stage2(c):
        near = (c + b) % 2
        far = 1 - near
        arrived(rbuf1.at[c], r1r.at[c])
        for i in range(2):
            fs[c, i] = acc[i, 2 * c + far, core] + rbuf1[c, i, far]
        rcopy(fs.at[c], rbuf2.at[c], r2s.at[c], r2r.at[c], partner).start()
        for i in range(2):
            acc[i, 2 * c + near, core] += rbuf1[c, i, near]

    def stage3(c):
        near = (c + b) % 2
        own = c * 2 + core
        dev = seq_of(own)
        arrived(rbuf2.at[c], r2r.at[c])
        for i in range(2):
            fb[c, i] = (acc[i, 2 * c + near, core] + rbuf2[c, i]).astype(BF)
        for i, (out, ssem, rsem) in enumerate(((dk_out, dks, dkr), (dv_out, dvs, dvr))):
            dst = out.at[:, cols(grp, W)]

            @pl.when(own != me)
            def _():
                rcopy(fb.at[c, i], dst, ssem.at[c], rsem.at[grp], dev).start()

            @pl.when(own == me)
            def _():
                pltpu.make_async_copy(fb.at[c, i], dst, rsem.at[grp]).start()

    def end(u):
        for p in range(2):
            n = 15 - 2 * u - p
            for h in range(2):
                i = 2 * p + h
                dqs[n, :, W * h:W * h + W] = dqt[:, W * i:W * i + W].T.astype(BF)
            dst = dq_out.at[:, cols(me, 256)]

            @pl.when(n != me)
            def _():
                rcopy(dqs.at[n], dst, dqss.at[n], dqr.at[me], seq_of(n)).start()

            @pl.when(n == me)
            def _():
                pltpu.make_async_copy(dqs.at[n], dst, dqr.at[me]).start()

    def clear(j):
        for i in range(2):
            acc[i, j] = jnp.zeros((2, W, W), F32)
    loop(16, clear)
    def first(xx):
        for zz in range(2):
            j = seq_in(xx * 4 + zz * 2 + core, 1 - b)
            arrived(kv.at[j], kvr.at[j])
            rcopy(kv.at[j], kv.at[j], f3s.at[2 * xx + zz], kvr.at[j], other).start()
        for zz in range(4):
            j = xx * 8 + zz * 2 + 1 - core
            arrived(kv.at[j], kvr.at[j])
        for i in range(2):
            c = 2 * xx + i
            kt[:, cols(c, CH)] = chunk_of(0, c).T
    loop(2, first)
    send_rows(g_in, gbuf, gs, gr)
    loop(4, first, 2)

    def phase_a(i):
        u = 7 - i
        prep_a(u)
        loop(i // 2, lambda j: part_a(2 * j, u, 2))

        @pl.when(i % 2 == 1)
        def _():
            part_a(i - 1, u)
        last_a(u)
    loop(8, phase_a)

    def phase_b(i):
        u = (i + 7) % 8
        prep_b(u)
        delta = delta_of(u)
        part_b(7 - u, u, delta)

        @pl.when(u < 7)
        def _():
            stage1(7 - u)

        def two(j):
            part_b(5 - u - 2 * j, u, delta, 2)

            @pl.when(j == 0)
            def _():
                stage2(7 - u)
        loop((7 - u) // 2, two)

        @pl.when(u % 2 == 0)
        def _():
            part_b(0, u, delta)
        end(u)

        @pl.when((u >= 2) & (u < 7))
        def _():
            stage3(9 - u)
    loop(8, phase_b)
    stage1(0)
    stage2(1)
    stage2(0)
    stage3(2)
    stage3(1)
    stage3(0)

    def finish(n):
        arrived(dq_out.at[:, cols(n, 256)], dqr.at[n])

        @pl.when(n != me)
        def _():
            rcopy(dqs.at[n], dqs.at[n], dqss.at[n], dqr.at[n], other).wait_send()
    loop(16, finish)

    def finish8(c):
        arrived(dk_out.at[:, cols(c, W)], dkr.at[c])
        arrived(dv_out.at[:, cols(c, W)], dvr.at[c])
        rcopy(fs.at[c], fs.at[c], r2s.at[c], r2r.at[c], other).wait_send()
        rcopy(rbuf1.at[c], rbuf1.at[c], r1s.at[c], r1r.at[c], other).wait_send()
        rcopy(kv.at[0], kv.at[0], f1s.at[c], kvr.at[0], other).wait_send()
        rcopy(kv.at[0], kv.at[0], f2s.at[c], kvr.at[0], other).wait_send()
        rcopy(kv.at[0], kv.at[0], f3s.at[c], kvr.at[0], other).wait_send()

        @pl.when(c * 2 + core != me)
        def _():
            rcopy(fb.at[c, 0], fb.at[c, 0], dks.at[c], dkr.at[c], other).wait_send()
            rcopy(fb.at[c, 1], fb.at[c, 1], dvs.at[c], dvr.at[c], other).wait_send()

        @pl.when(c >= 1)
        def _():
            rcopy(kvs.at[0], kvs.at[0], s1s.at[c], kvr.at[0], other).wait_send()
    loop(8, finish8)

    def finish15(k):
        rcopy(qbuf.at[0], qbuf.at[0], qs.at[k], qr.at[0], other).wait_send()
        rcopy(gbuf.at[0], gbuf.at[0], gs.at[k], gr.at[0], other).wait_send()
        rcopy(de.at[0], de.at[0], des.at[k], der.at[0], other).wait_send()
    loop(16, finish15, 1)


def per_device(q, kc, ks, vc, vs, o, g):
    any_ = pl.BlockSpec(memory_space=pl.ANY)
    vm, dma = pltpu.VMEM, pltpu.SemaphoreType.DMA
    rows, qc = q.shape
    kc_cols = kc.shape[1]
    return pl.pallas_call(
        kernel,
        out_shape=[vm(q.shape, BF), vm(kc.shape, BF), vm(vc.shape, BF)],
        in_specs=[any_] * 7,
        out_specs=[pl.BlockSpec(memory_space=pltpu.VMEM)] * 3,
        scratch_shapes=[
            vm((rows, qc), BF), vm((rows, qc), BF), vm((rows, kc_cols), BF), vm((rows, kc_cols), BF),
            vm((1, 8), BF), vm((1, 8), BF), vm((W, W), F32), vm((8, 2, W, W), BF),
            vm((32, 2, W, W), BF), vm((W, 32 * W), BF),
            vm((16, W, 256), BF), vm((16, W, 256), BF), vm((16, 8, W), F32),
            vm((36, CH, 512), F32),
            vm((W, 512), BF), vm((W, 512), BF), vm((512, W), BF), vm((512, W), BF),
            vm((W, 512), F32), vm((2, 8, 512), F32), vm((8, 1, 512), F32),
            vm((2, 16, 2, W, W), F32), vm((16, W, 256), BF),
            vm((8, 2, 2, W, W), F32), vm((8, 2, W, W), F32), vm((8, 2, W, W), F32),
            vm((8, 2, W, W), BF),
            dma((6,)), dma((8,)), dma((32,)), dma((8,)), dma((8,)), dma((8,)),
            dma((16,)), dma((16,)), dma((16,)), dma((16,)), dma((16,)), dma((16,)),
            dma((16,)), dma((16,)),
            dma((8,)), dma((8,)), dma((8,)), dma((8,)), dma((8,)), dma((8,)), dma((8,)), dma((8,)),
        ],
        compiler_params=pltpu.CompilerParams(
            collective_id=0, has_side_effects=True, vmem_limit_bytes=62 * 2**20
        ),
        cost_estimate=pl.CostEstimate(
            flops=11_000_000_000, bytes_accessed=8_000_000, transcendentals=18_000_000
        ),
    )(q, kc, ks, vc, vs, o, g)


def solution(mesh):
    spec = P(("dp", "seq"), None)
    return jax.shard_map(
        per_device, mesh=mesh, in_specs=(spec,) * 7, out_specs=(spec,) * 3, check_vma=False
    )
```
